256 devices in a mesh: pair: 16 (over z_lo, y), aux: 16 (over z_hi, x, core).
Axes of the slice: x: 4, y: 4, z: 8 (z_hi: 2, z_lo: 4; z = z_hi * 4 + z_lo), core: 2. Of those that a mesh axis runs over, the one named last changes fastest.
Arguments:
- amplitudes: float32 [896, 16, 896], P('aux', 'pair'), may hold values from -6 to 6
- fitting: float32 [16, 896, 896], P('aux', 'pair'), may hold values from -0.09375 to 0.09375
Outputs:
- ladder: float32 [896, 16, 896], P('aux', 'pair')
The draws below stay inside these ranges and needn't reach their ends.
All inputs are finite; a program needn't handle non-finite values.
Results may differ from the reference program's by a relative error of at most 0.0001.
Values sent between devices are 32-bit elements; how exact they have to be, the bound alone decides.
No kernel may reach another device: no remote copies, remote signals or barrier semaphores. Data moves between devices by JAX's collectives and lax.ppermute only.
A program may use at most 64 MiB of HBM per device.

```python
import jax
import jax.numpy as jnp
from jax import lax

V = 896
NPAIRS = 16
NFIT = 16


def level_of(own_key, extent, split, least, largest):
    gain, own = 1.0, jax.random.fold_in(own_key, 6)
    for position, parts in split:
        draws = jnp.exp(jax.random.uniform(jax.random.fold_in(own, position), (parts,), jnp.float32, least / len(split), largest / len(split)))
        gain = gain * jnp.repeat(draws, extent[position] // parts).reshape([-1 if axis == position else 1 for axis in range(len(extent))])
    return gain


def gaussian(stream_key, extent, width, reach, pieces=(), dtype=jnp.bfloat16):
    entries = width * jax.random.normal(stream_key, extent, jnp.float32)
    if pieces:
        entries = entries * level_of(stream_key, extent, pieces, -0.22, 0.18)
    return jnp.clip(entries, -reach, reach).astype(dtype)


def setup_inputs(seed: int = 0) -> dict:
    splits = jax.random.split(jax.random.key(seed), 3)
    amplitudes = gaussian(splits[0], (V, NPAIRS, V), 1.0, 6.0, ((0, 16), (1, 16)), jnp.float32)
    fitting = gaussian(splits[1], (NFIT, V, V), (V * 4) ** -0.5, 0.09375, ((0, 16), (1, 16)), jnp.float32)
    return dict(amplitudes=amplitudes, fitting=fitting)


def reference(amplitudes, fitting):
    flat = amplitudes.reshape(V * NPAIRS, V)

    def step(total, matrix):
        half = jnp.dot(flat, matrix.T, precision=lax.Precision.HIGHEST, preferred_element_type=jnp.float32)
        half = half.reshape(V, NPAIRS * V)
        return total + jnp.dot(matrix, half, precision=lax.Precision.HIGHEST, preferred_element_type=jnp.float32), None

    total, _ = lax.scan(step, jnp.zeros((V, NPAIRS * V), jnp.float32), fitting)
    return total.reshape(V, NPAIRS, V)
```

```python
import jax
import jax.numpy as jnp
from jax import lax
from jax.experimental import pallas as pl
from jax.experimental.pallas import tpu as pltpu
from jax.sharding import PartitionSpec as P

NZL, NY, NZH, NX, NC = 4, 4, 2, 4, 2
V = 896
ROWS = 56
TILE = 128


def pair_permute(value, target):
    steps = []
    for zl in range(NZL):
        for y in range(NY):
            tz, ty = target(zl, y)
            steps.append((zl * NY + y, (tz % NZL) * NY + ty % NY))
    return lax.ppermute(value, "pair", steps)


def aux_permute(value, target):
    steps = []
    for zh in range(NZH):
        for x in range(NX):
            for c in range(NC):
                th, tx, tc = target(zh, x, c)
                steps.append(((zh * NX + x) * NC + c, ((th % NZH) * NX + tx % NX) * NC + tc % NC))
    return lax.ppermute(value, "aux", steps)


def split(value):
    high = value.astype(jnp.bfloat16)
    low = (value - high.astype(jnp.float32)).astype(jnp.bfloat16)
    return high, low


def ladder_kernel(place_ref, *refs):
    t_refs, b_refs = refs[:10], refs[10:26]
    keep_ref, send_ref = refs[26:28]
    t32, b32, t_hi, t_lo, b_hi, b_lo, sem = refs[28:]
    zl, y, zh, x, core = (place_ref[i] for i in range(5))
    copies = []
    for index in range(8):
        far, k = divmod(index, 4)
        block = ((zh + far) % NZH) * 8 + ((x - k + NX) % NX) * 2
        mine = pl.multiple_of((block + core) * ROWS, 8)
        other = pl.multiple_of((block + 1 - core) * ROWS, 8)
        copies.append(pltpu.make_async_copy(t_refs[index], t32.at[pl.ds(mine, ROWS)], sem.at[index]))
        copies.append(
            pltpu.make_async_copy(t_refs[8 + far].at[pl.ds(k * ROWS, ROWS)], t32.at[pl.ds(other, ROWS)], sem.at[8 + index])
        )
    for index in range(16):
        k, j = divmod(index, 4)
        row = pl.multiple_of(((zl ^ k) * NY + (y - j + NY) % NY) * ROWS, 8)
        copies.append(pltpu.make_async_copy(b_refs[index], b32.at[pl.ds(row, ROWS)], sem.at[16 + index]))
    for copy in copies:
        copy.start()
    for copy in copies:
        copy.wait()

    def load(i, carry):
        rows = pl.ds(pl.multiple_of(i * TILE, TILE), TILE)
        t_hi[rows], t_lo[rows] = split(t32[rows])
        b_hi[rows], b_lo[rows] = split(b32[rows])
        return carry

    lax.fori_loop(0, V // TILE, load, 0)

    def product(i, carry):
        rows = pl.ds(pl.multiple_of(i * TILE, TILE), TILE)
        nn = (((1,), (0,)), ((), ()))
        nt = (((1,), (1,)), ((), ()))

        def dot(left, right, dims):
            return lax.dot_general(left, right, dims, preferred_element_type=jnp.float32)

        high, low = b_hi[rows], b_lo[rows]
        g = dot(low, t_hi[...], nn) + dot(high, t_lo[...], nn) + dot(high, t_hi[...], nn)
        high, low = split(g)
        t32[rows] = dot(low, b_hi[...], nt) + dot(high, b_lo[...], nt) + dot(high, b_hi[...], nt)
        return carry

    lax.fori_loop(0, V // TILE, product, 0)

    copies = []
    for index in range(8):
        far, k = divmod(index, 4)
        block = ((zh + 1 - far) % NZH) * 8 + ((x + k) % NX) * 2
        mine = pl.multiple_of((block + core) * ROWS, 8)
        other = pl.multiple_of((block + 1 - core) * ROWS, 8)
        copies.append(pltpu.make_async_copy(t32.at[pl.ds(mine, ROWS)], keep_ref.at[index], sem.at[index]))
        copies.append(pltpu.make_async_copy(t32.at[pl.ds(other, ROWS)], send_ref.at[index], sem.at[8 + index]))
    for copy in copies:
        copy.start()
    for copy in copies:
        copy.wait()


def ladder_call(place, t_parts, b_parts):
    any_spec = pl.BlockSpec(memory_space=pl.ANY)
    out = jax.ShapeDtypeStruct((8, ROWS, V), jnp.float32)
    return pl.pallas_call(
        ladder_kernel,
        out_shape=(out, out),
        in_specs=[pl.BlockSpec(memory_space=pltpu.SMEM)] + [any_spec] * 26,
        out_specs=(any_spec, any_spec),
        scratch_shapes=[
            pltpu.VMEM((V, V), jnp.float32),
            pltpu.VMEM((V, V), jnp.float32),
            pltpu.VMEM((V, V), jnp.bfloat16),
            pltpu.VMEM((V, V), jnp.bfloat16),
            pltpu.VMEM((V, V), jnp.bfloat16),
            pltpu.VMEM((V, V), jnp.bfloat16),
            pltpu.SemaphoreType.DMA((32,)),
        ],
        compiler_params=pltpu.CompilerParams(vmem_limit_bytes=40 * 1024 * 1024),
        cost_estimate=pl.CostEstimate(flops=4 * 3 * V**3, bytes_accessed=4 * 4 * V * V, transcendentals=0),
        name="ladder",
    )(place, *t_parts, *b_parts)


def per_device(amplitudes, fitting):
    pair, aux = lax.axis_index("pair"), lax.axis_index("aux")
    place = jnp.stack([pair // NY, pair % NY, aux // 8, aux // 2 % NX, aux % 2]).astype(jnp.int32)
    amp = amplitudes.reshape(ROWS, V)
    fit = fitting.reshape(ROWS, V)

    with jax.named_scope("gather_fit"):
        shards = [fit] + [pair_permute(fit, lambda zl, y, k=k: (zl ^ k, y)) for k in (1, 2, 3)]
        b_parts = []
        for shard in shards:
            b_parts.append(shard)
            for j in (1, 2, 3):
                b_parts.append(pair_permute(shard, lambda zl, y, j=j: (zl, y + j)))

    with jax.named_scope("gather_amp"):
        far = aux_permute(amp, lambda zh, x, c: (zh + 1, x, c))
        t_parts, stacks = [], []
        for shard in (amp, far):
            parts = [shard] + [aux_permute(shard, lambda zh, x, c, k=k: (zh, x + k, c)) for k in (1, 2, 3)]
            t_parts += parts
            stacks.append(aux_permute(jnp.concatenate(parts), lambda zh, x, c: (zh, x, c + 1)))
        t_parts += stacks

    keep, send = ladder_call(place, t_parts, b_parts)

    with jax.named_scope("reduce"):
        halves = []
        for far in (0, 1):
            blocks = slice(4 * far, 4 * far + 4)
            got = aux_permute(send[blocks], lambda zh, x, c: (zh, x, c + 1))
            both = keep[blocks] + got
            total = both[0]
            for k in (1, 2, 3):
                total = total + aux_permute(both[k], lambda zh, x, c, k=k: (zh, x + k, c))
            halves.append(total)
        result = halves[1] + aux_permute(halves[0], lambda zh, x, c: (zh + 1, x, c))
    return result.reshape(ROWS, 1, V)


def solution(mesh):
    in_specs = (P("aux", "pair", None), P("aux", "pair", None))
    out_specs = P("aux", "pair", None)
    return jax.shard_map(
        per_device, mesh=mesh, in_specs=in_specs, out_specs=out_specs, check_vma=False
    )
```

```python
import jax
import jax.numpy as jnp
from jax import lax
from jax.experimental import pallas as pl
from jax.experimental.pallas import tpu as pltpu
from jax.sharding import PartitionSpec as P

NZL, NY, NZH, NX, NC = 4, 4, 2, 4, 2
V = 896
HALF = 448
ROWS = 56
NN = (((1,), (0,)), ((), ()))
NT = (((1,), (1,)), ((), ()))
ANY = pl.BlockSpec(memory_space=pl.ANY)
SMEM = pl.BlockSpec(memory_space=pltpu.SMEM)


def pair_permute(value, target):
    steps = []
    for zl in range(NZL):
        for y in range(NY):
            tz, ty = target(zl, y)
            steps.append((zl * NY + y, (tz % NZL) * NY + ty % NY))
    return lax.ppermute(value, "pair", steps)


def aux_permute(value, target):
    steps = []
    for zh in range(NZH):
        for x in range(NX):
            for c in range(NC):
                th, tx, tc = target(zh, x, c)
                steps.append(((zh * NX + x) * NC + c, ((th % NZH) * NX + tx % NX) * NC + tc % NC))
    return lax.ppermute(value, "aux", steps)


def swap_core(value):
    return aux_permute(value, lambda zh, x, c: (zh, x, 1 - c))


def split(value):
    high = value.astype(jnp.bfloat16)
    low = (value - high.astype(jnp.float32)).astype(jnp.bfloat16)
    return high, low


def product(left, right, dims):
    def dot(a, b):
        return lax.dot_general(a, b, dims, preferred_element_type=jnp.float32)

    return dot(left[1], right[0]) + dot(left[0], right[1]) + dot(left[0], right[0])


def run_copies(copies):
    for copy in copies:
        copy.start()
    for copy in copies:
        copy.wait()


def fit_copies(refs, target, zl, y, sem, first):
    both, below, above, low2, high2 = refs
    places = [(both, 0, 0, 0), (both, 1, 1, 0), (below, 0, 0, 3), (below, 1, 1, 3)]
    places += [(above, 0, 0, 1), (above, 1, 1, 1), (low2, 0, 0, 2), (high2, 0, 1, 2)]
    copies = []
    for index, (ref, part, k, j) in enumerate(places):
        row = pl.multiple_of(((zl + k) % 2) * 224 + ((y + j) % NY) * ROWS, 8)
        copies.append(
            pltpu.make_async_copy(ref.at[pl.ds(part * ROWS, ROWS)], target.at[pl.ds(row, ROWS)], sem.at[first + index])
        )
    return copies


def amp_copies(refs, target, zh, x, core, sem):
    mine, other, beside, across, relay, relay_other = refs
    step = 2 * core - 1
    places = []
    for far in (0, 1):
        places += [(mine, far, far, 0, core), (other, far, far, 0, 1 - core)]
        places += [(beside, far, far, step, core), (beside, 2 + far, far, step, 1 - core)]
        places += [(across, far, far, -step, 1 - core), (across, 2 + far, far, -step, core)]
        places += [(relay, far, far, 2, core), (relay_other, far, far, 2, 1 - core)]
    copies = []
    for index, (ref, part, far, dx, c) in enumerate(places):
        row = pl.multiple_of((((zh + far) % NZH) * 8 + ((x + dx + NX) % NX) * 2 + c) * ROWS, 8)
        copies.append(
            pltpu.make_async_copy(ref.at[pl.ds(part * ROWS, ROWS)], target.at[pl.ds(row, ROWS)], sem.at[index])
        )
    return copies


def first_kernel(place_ref, *refs):
    t_refs, b_refs = refs[:6], refs[6:11]
    t_hi, t_lo, b_hi, b_lo, g_hi, g_lo = refs[11:17]
    t32, b32, sem = refs[17:]
    zl, y, zh, x, core = (place_ref[i] for i in range(5))
    run_copies(amp_copies(t_refs, t32, zh, x, core, sem) + fit_copies(b_refs, b32, zl, y, sem, 16))
    for row in range(0, V, 128):
        rows = slice(row, row + 128)
        t_hi[rows], t_lo[rows] = split(t32[rows])
    for row in range(0, HALF, 64):
        rows = slice(row, row + 64)
        b_hi[rows], b_lo[rows] = split(b32[rows])
    g_hi[...], g_lo[...] = split(product((b_hi[...], b_lo[...]), (t_hi[...], t_lo[...]), NN))


def out_copies(total, keep_ref, send_ref, half, x, core, sem):
    copies = []
    for k in range(NX):
        block = ((x + k) % NX) * 2
        mine = pl.multiple_of((block + core) * ROWS, 8)
        other = pl.multiple_of((block + 1 - core) * ROWS, 8)
        copies.append(pltpu.make_async_copy(total.at[pl.ds(mine, ROWS)], keep_ref.at[k], sem.at[k]))
        copies.append(pltpu.make_async_copy(total.at[pl.ds(other, ROWS)], send_ref.at[k], sem.at[NX + k]))
    return copies


def second_kernel(place_ref, *refs):
    t_hi, t_lo, ba_hi, ba_lo, ga_hi, ga_lo = refs[:6]
    b_refs = refs[6:11]
    b_hi, b_lo, g_hi, g_lo, keep_ref, send_ref = refs[11:17]
    b32, total, sem = refs[17:]
    zl, y, zh, x, core = (place_ref[i] for i in range(5))
    run_copies(fit_copies(b_refs, b32, zl, y, sem, 0))
    upper = zl // 2
    rows_a = pl.ds(pl.multiple_of(upper * HALF, HALF), HALF)
    rows_b = pl.ds(pl.multiple_of((1 - upper) * HALF, HALF), HALF)
    high, low = split(b32[...])
    b_hi[rows_b], b_lo[rows_b] = high, low
    g_hi[rows_b], g_lo[rows_b] = split(product((high, low), (t_hi[...], t_lo[...]), NN))
    b_hi[rows_a], b_lo[rows_a] = ba_hi[...], ba_lo[...]
    g_hi[rows_a], g_lo[rows_a] = ga_hi[...], ga_lo[...]
    rows = pl.ds(pl.multiple_of((1 - zh) * HALF, HALF), HALF)
    total[...] = product((g_hi[rows], g_lo[rows]), (b_hi[...], b_lo[...]), NT)
    run_copies(out_copies(total, keep_ref, send_ref, 1 - zh, x, core, sem))


def third_kernel(place_ref, b_hi, b_lo, g_hi, g_lo, keep_ref, send_ref, total, sem):
    zh, x, core = (place_ref[i] for i in range(2, 5))
    rows = pl.ds(pl.multiple_of(zh * HALF, HALF), HALF)
    total[...] = product((g_hi[rows], g_lo[rows]), (b_hi[...], b_lo[...]), NT)
    run_copies(out_copies(total, keep_ref, send_ref, zh, x, core, sem))


def call(kernel, outs, out_specs, scratch, args, in_specs, flops, moved, name):
    return pl.pallas_call(
        kernel,
        out_shape=outs,
        in_specs=in_specs,
        out_specs=out_specs,
        scratch_shapes=scratch,
        compiler_params=pltpu.CompilerParams(vmem_limit_bytes=36 * 1024 * 1024),
        cost_estimate=pl.CostEstimate(flops=flops, bytes_accessed=moved, transcendentals=0),
        name=name,
    )(*args)


def per_device(amplitudes, fitting):
    pair, aux = lax.axis_index("pair"), lax.axis_index("aux")
    place = jnp.stack([pair // NY, pair % NY, aux // 8, aux // 2 % NX, aux % 2]).astype(jnp.int32)
    amp = amplitudes.reshape(ROWS, V)
    fit = fitting.reshape(ROWS, V)

    def spread(both):
        below = pair_permute(both, lambda zl, y: (zl, y + 1))
        above = pair_permute(both, lambda zl, y: (zl, y - 1))
        low2 = pair_permute(below[:ROWS], lambda zl, y: (zl, y + 1))
        high2 = pair_permute(above[ROWS:], lambda zl, y: (zl, y - 1))
        return [both, below, above, low2, high2]

    with jax.named_scope("gather_fit"):
        near = pair_permute(fit, lambda zl, y: (zl ^ 1, y))
        far = [pair_permute(fit, lambda zl, y, k=k: (zl ^ k, y)) for k in (2, 3)]
        fit_a = spread(jnp.concatenate([fit, near]))
        fit_b = spread(jnp.concatenate(far))

    with jax.named_scope("gather_amp"):
        mine = jnp.concatenate([amp, aux_permute(amp, lambda zh, x, c: (1 - zh, x, c))])
        other = swap_core(mine)
        chip = jnp.concatenate([mine, other])
        beside = aux_permute(chip, lambda zh, x, c: (zh, x + 1 - 2 * c, c))
        across = swap_core(beside)
        relay = aux_permute(beside[: 2 * ROWS], lambda zh, x, c: (zh, x + 1 - 2 * c, c))
        amps = [mine, other, beside, across, relay, swap_core(relay)]

    VMEM = pl.BlockSpec(memory_space=pltpu.VMEM)
    whole = jax.ShapeDtypeStruct((V, V), jnp.bfloat16)
    half = jax.ShapeDtypeStruct((HALF, V), jnp.bfloat16)
    blocks = jax.ShapeDtypeStruct((NX, ROWS, V), jnp.float32)
    cube = V**3
    first = call(
        first_kernel,
        (whole, whole, half, half, half, half),
        (VMEM,) * 6,
        [pltpu.VMEM((V, V), jnp.float32), pltpu.VMEM((HALF, V), jnp.float32), pltpu.SemaphoreType.DMA((24,))],
        (place, *amps, *fit_a),
        [SMEM] + [ANY] * 11,
        3 * cube,
        12 * V * V,
        "first_half",
    )
    second = call(
        second_kernel,
        (whole, whole, whole, whole, blocks, blocks),
        (VMEM,) * 4 + (ANY,) * 2,
        [pltpu.VMEM((HALF, V), jnp.float32), pltpu.VMEM((HALF, V), jnp.float32), pltpu.SemaphoreType.DMA((8,))],
        (place, *first, *fit_b),
        [SMEM] + [VMEM] * 6 + [ANY] * 5,
        6 * cube,
        20 * V * V,
        "second_half",
    )
    b_hi, b_lo, g_hi, g_lo, *far_rows = second
    near_rows = call(
        third_kernel,
        (blocks, blocks),
        (ANY,) * 2,
        [pltpu.VMEM((HALF, V), jnp.float32), pltpu.SemaphoreType.DMA((8,))],
        (place, b_hi, b_lo, g_hi, g_lo),
        [SMEM] + [VMEM] * 4,
        3 * cube,
        12 * V * V,
        "near_rows",
    )

    def reduce_x(keep, send):
        both = keep + swap_core(send)
        total = both[0]
        for k in (1, 2, 3):
            total = total + aux_permute(both[k], lambda zh, x, c, k=k: (zh, x + k, c))
        return total

    with jax.named_scope("reduce"):
        far_sum = aux_permute(reduce_x(*far_rows), lambda zh, x, c: (1 - zh, x, c))
        result = reduce_x(*near_rows) + far_sum
    return result.reshape(ROWS, 1, V)


def solution(mesh):
    in_specs = (P("aux", "pair", None), P("aux", "pair", None))
    out_specs = P("aux", "pair", None)
    return jax.shard_map(
        per_device, mesh=mesh, in_specs=in_specs, out_specs=out_specs, check_vma=False
    )
```

```python
import jax
import jax.numpy as jnp
from jax import lax
from jax.experimental import pallas as pl
from jax.experimental.pallas import tpu as pltpu
from jax.sharding import PartitionSpec as P

NZL, NY, NZH, NX, NC = 4, 4, 2, 4, 2
V = 896
HALF = 448
ROWS = 56
NN = (((1,), (0,)), ((), ()))
NT = (((1,), (1,)), ((), ()))
ANY = pl.BlockSpec(memory_space=pl.ANY)
SMEM = pl.BlockSpec(memory_space=pltpu.SMEM)


def pair_permute(value, target):
    steps = []
    for zl in range(NZL):
        for y in range(NY):
            tz, ty = target(zl, y)
            steps.append((zl * NY + y, (tz % NZL) * NY + ty % NY))
    return lax.ppermute(value, "pair", steps)


def aux_permute(value, target):
    steps = []
    for zh in range(NZH):
        for x in range(NX):
            for c in range(NC):
                th, tx, tc = target(zh, x, c)
                steps.append(((zh * NX + x) * NC + c, ((th % NZH) * NX + tx % NX) * NC + tc % NC))
    return lax.ppermute(value, "aux", steps)


def swap_core(value):
    return aux_permute(value, lambda zh, x, c: (zh, x, 1 - c))


def split(value):
    high = value.astype(jnp.bfloat16)
    low = (value - high.astype(jnp.float32)).astype(jnp.bfloat16)
    return high, low


def product(left, right, dims):
    def dot(a, b):
        return lax.dot_general(a, b, dims, preferred_element_type=jnp.float32)

    return dot(left[1], right[0]) + dot(left[0], right[1]) + dot(left[0], right[0])


def run_copies(copies):
    for copy in copies:
        copy.start()
    for copy in copies:
        copy.wait()


def fit_copies(places, target, zl, y, sem, first):
    copies = []
    for index, (ref, part, k, j) in enumerate(places):
        row = pl.multiple_of(((zl ^ k) * NY + (y + j) % NY) * ROWS, 8)
        copies.append(
            pltpu.make_async_copy(ref.at[pl.ds(part * ROWS, ROWS)], target.at[pl.ds(row, ROWS)], sem.at[first + index])
        )
    return copies


def amp_copies(refs, target, zh, x, core, sem):
    own, far, beside, beside_far, across, across_far, relay, relay_other = refs
    step = 2 * core - 1
    places = []
    for f, here, there, back in ((0, own, beside, across), (1, far, beside_far, across_far)):
        places += [(here, 0, f, 0, core), (here, 1, f, 0, 1 - core)]
        places += [(there, 0, f, step, core), (there, 1, f, step, 1 - core)]
        places += [(back, 0, f, -step, 1 - core), (back, 1, f, -step, core)]
        places += [(relay, f, f, 2, core), (relay_other, f, f, 2, 1 - core)]
    copies = []
    for index, (ref, part, f, dx, c) in enumerate(places):
        row = pl.multiple_of((((zh + f) % NZH) * 8 + ((x + dx + NX) % NX) * 2 + c) * ROWS, 8)
        copies.append(
            pltpu.make_async_copy(ref.at[pl.ds(part * ROWS, ROWS)], target.at[pl.ds(row, ROWS)], sem.at[index])
        )
    return copies


def ladder_kernel(place_ref, *refs):
    t_refs, own = refs[:8], refs[8:12]
    both, below, above, three, up3, down3, across3 = refs[12:19]
    outs = refs[19:23]
    t32, b32, t_hi, t_lo, b_hi, b_lo, g_hi, g_lo, total, sem, out_sem = refs[23:]
    zl, y, zh, x, core = (place_ref[i] for i in range(5))
    places = [(ref, 0, 0, j) for ref, j in zip(own, (0, 3, 1, 2))]
    for part in (0, 1):
        places += [(both, part, part + 1, 0), (below, part, part + 1, 3), (above, part, part + 1, 1)]
    places += [(three, 0, 3, 0), (up3, 0, 3, 3), (up3, 1, 2, 2), (down3, 0, 3, 1), (down3, 1, 1, 2), (across3, 0, 3, 2)]
    amp = amp_copies(t_refs, t32, zh, x, core, sem)
    fit = fit_copies(places, b32, zl, y, sem, 16)
    for copy in amp + fit:
        copy.start()
    for copy in amp:
        copy.wait()
    for row in range(0, V, 128):
        rows = slice(row, row + 128)
        t_hi[rows], t_lo[rows] = split(t32[rows])
    for copy in fit:
        copy.wait()
    for row in (0, HALF):
        rows = slice(row, row + HALF)
        b_hi[rows], b_lo[rows] = split(b32[rows])
        g_hi[rows], g_lo[rows] = split(product((b_hi[rows], b_lo[rows]), (t_hi[...], t_lo[...]), NN))
    copies = []
    for far in (1, 0):
        half = (zh + far) % NZH
        rows = pl.ds(pl.multiple_of(half * HALF, HALF), HALF)
        total[far] = product((g_hi[rows], g_lo[rows]), (b_hi[...], b_lo[...]), NT)
        for k in range(NX):
            block = ((x + k) % NX) * 2
            for n, c in enumerate((core, 1 - core)):
                row = pl.multiple_of((block + c) * ROWS, 8)
                copies.append(
                    pltpu.make_async_copy(
                        total.at[far, pl.ds(row, ROWS)], outs[2 * (1 - far) + n].at[k], out_sem.at[far, n, k]
                    )
                )
                copies[-1].start()
    for copy in copies:
        copy.wait()


def call(kernel, outs, out_specs, scratch, args, in_specs, flops, moved, name):
    return pl.pallas_call(
        kernel,
        out_shape=outs,
        in_specs=in_specs,
        out_specs=out_specs,
        scratch_shapes=scratch,
        compiler_params=pltpu.CompilerParams(vmem_limit_bytes=52 * 1024 * 1024),
        cost_estimate=pl.CostEstimate(flops=flops, bytes_accessed=moved, transcendentals=0),
        name=name,
    )(*args)


def per_device(amplitudes, fitting):
    pair, aux = lax.axis_index("pair"), lax.axis_index("aux")
    place = jnp.stack([pair // NY, pair % NY, aux // 8, aux // 2 % NX, aux % 2]).astype(jnp.int32)
    fit = fitting.reshape(ROWS, V)

    def up(value):
        return pair_permute(value, lambda zl, y: (zl, y + 1))

    def down(value):
        return pair_permute(value, lambda zl, y: (zl, y - 1))

    def beside_x(value):
        return aux_permute(value, lambda zh, x, c: (zh, x + 1 - 2 * c, c))

    def pack(*parts):
        return jnp.concatenate(parts)

    tie = lax.optimization_barrier
    amp = amplitudes.reshape(ROWS, V)
    with jax.named_scope("gather"):
        near = pair_permute(fit, lambda zl, y: (zl ^ 1, y))
        two = pair_permute(fit, lambda zl, y: (zl ^ 2, y))
        own = pack(amp, swap_core(amp))
        fit_0 = up(fit), down(fit)
        beside = beside_x(own)
        amp_late, beside, fit_0, near, two = tie((amp, beside, fit_0, near, two))

        far = aux_permute(amp_late, lambda zh, x, c: (1 - zh, x, c))
        three = pair_permute(two, lambda zl, y: (zl ^ 1, y))
        both = pack(near, two)
        below, above = up(both), down(both)
        low = up(fit_0[0])
        low, below, above, three, far = tie((low, below, above, three, far))

        far_amp, far = far, pack(far, swap_core(far))
        beside_far, beside = tie((beside_x(far), beside))
        up3 = up(pack(three, below[ROWS:]))
        down3 = down(pack(three, above[:ROWS]))
        across3 = pair_permute(three, lambda zl, y: (zl, y + 2))
        relay = aux_permute(pack(amp, far_amp), lambda zh, x, c: (zh, x + 2, c))
        amps = [own, far, beside, beside_far, swap_core(beside), swap_core(beside_far), relay, swap_core(relay)]
        fits = [fit, *fit_0, low, both, below, above, three, up3, down3, across3]

    blocks = jax.ShapeDtypeStruct((NX, ROWS, V), jnp.float32)
    vmem = pltpu.VMEM
    sems = pltpu.SemaphoreType.DMA
    far_keep, far_send, near_keep, near_send = call(
        ladder_kernel,
        (blocks,) * 4,
        (ANY,) * 4,
        [vmem((V, V), jnp.float32)] * 2
        + [vmem((V, V), jnp.bfloat16)] * 6
        + [vmem((2, HALF, V), jnp.float32), sems((32,)), sems((2, 2, NX))],
        (place, *amps, *fits),
        [SMEM] + [ANY] * 19,
        12 * V**3,
        16 * V * V,
        "ladder",
    )

    def reduce_x(keep, send):
        both = keep + swap_core(send)
        total = both[0]
        for k in (1, 2, 3):
            total = total + aux_permute(both[k], lambda zh, x, c, k=k: (zh, x + k, c))
        return total

    with jax.named_scope("reduce"):
        far_sum = aux_permute(reduce_x(far_keep, far_send), lambda zh, x, c: (1 - zh, x, c))
        result = reduce_x(near_keep, near_send) + far_sum
    return result.reshape(ROWS, 1, V)


def solution(mesh):
    in_specs = (P("aux", "pair", None), P("aux", "pair", None))
    out_specs = P("aux", "pair", None)
    return jax.shard_map(
        per_device, mesh=mesh, in_specs=in_specs, out_specs=out_specs, check_vma=False
    )
```

```python
import jax
import jax.numpy as jnp
from jax import lax
from jax.experimental import pallas as pl
from jax.experimental.pallas import tpu as pltpu
from jax.sharding import PartitionSpec as P

NZL, NY, NZH, NX, NC = 4, 4, 2, 4, 2
V = 896
HALF = 448
ROWS = 56
NN = (((1,), (0,)), ((), ()))
NT = (((1,), (1,)), ((), ()))
ANY = pl.BlockSpec(memory_space=pl.ANY)
SMEM = pl.BlockSpec(memory_space=pltpu.SMEM)


def pair_permute(value, target):
    steps = []
    for zl in range(NZL):
        for y in range(NY):
            tz, ty = target(zl, y)
            steps.append((zl * NY + y, (tz % NZL) * NY + ty % NY))
    return lax.ppermute(value, "pair", steps)


def aux_permute(value, target):
    steps = []
    for zh in range(NZH):
        for x in range(NX):
            for c in range(NC):
                th, tx, tc = target(zh, x, c)
                steps.append(((zh * NX + x) * NC + c, ((th % NZH) * NX + tx % NX) * NC + tc % NC))
    return lax.ppermute(value, "aux", steps)


def swap_core(value):
    return aux_permute(value, lambda zh, x, c: (zh, x, 1 - c))


def split(value):
    high = value.astype(jnp.bfloat16)
    low = (value - high.astype(jnp.float32)).astype(jnp.bfloat16)
    return high, low


def product(left, right, dims):
    def dot(a, b):
        return lax.dot_general(a, b, dims, preferred_element_type=jnp.float32)

    return dot(left[1], right[0]) + dot(left[0], right[1]) + dot(left[0], right[0])


def run_copies(copies):
    for copy in copies:
        copy.start()
    for copy in copies:
        copy.wait()


def fit_copies(places, target, zl, y, sem, first):
    copies = []
    for index, (ref, part, k, j) in enumerate(places):
        row = pl.multiple_of(((zl ^ k) * NY + (y + j) % NY) * ROWS, 8)
        copies.append(
            pltpu.make_async_copy(ref.at[pl.ds(part * ROWS, ROWS)], target.at[pl.ds(row, ROWS)], sem.at[first + index])
        )
    return copies


def amp_copies(refs, target, zh, x, core, sem):
    own, far, beside, beside_far, across, across_far, relay, relay_other = refs
    step = 2 * core - 1
    places = []
    for f, here, there, back in ((0, own, beside, across), (1, far, beside_far, across_far)):
        places += [(here, 0, f, 0, core), (here, 1, f, 0, 1 - core)]
        places += [(there, 0, f, step, core), (there, 1, f, step, 1 - core)]
        places += [(back, 0, f, -step, 1 - core), (back, 1, f, -step, core)]
        places += [(relay, f, f, 2, core), (relay_other, f, f, 2, 1 - core)]
    copies = []
    for index, (ref, part, f, dx, c) in enumerate(places):
        row = pl.multiple_of((((zh + f) % NZH) * 8 + ((x + dx + NX) % NX) * 2 + c) * ROWS, 8)
        copies.append(
            pltpu.make_async_copy(ref.at[pl.ds(part * ROWS, ROWS)], target.at[pl.ds(row, ROWS)], sem.at[index])
        )
    return copies


def ladder_kernel(place_ref, *refs):
    t_refs, own = refs[:8], refs[8:12]
    both, below, above, three, up3, down3, across3 = refs[12:19]
    outs = refs[19:23]
    t32, b32, t_hi, t_lo, b_hi, b_lo, g_hi, g_lo, total, sem, out_sem = refs[23:]
    zl, y, zh, x, core = (place_ref[i] for i in range(5))
    places = [(ref, 0, 0, j) for ref, j in zip(own, (0, 3, 1, 2))]
    for part in (0, 1):
        places += [(both, part, part + 1, 0), (below, part, part + 1, 3), (above, part, part + 1, 1)]
    places += [(three, 0, 3, 0), (up3, 0, 3, 3), (up3, 1, 2, 2), (down3, 0, 3, 1), (down3, 1, 1, 2), (across3, 0, 3, 2)]
    amp = amp_copies(t_refs, t32, zh, x, core, sem)
    fit = fit_copies(places, b32, zl, y, sem, 16)
    for copy in amp + fit:
        copy.start()
    for copy in amp:
        copy.wait()
    for row in range(0, V, 128):
        rows = slice(row, row + 128)
        t_hi[rows], t_lo[rows] = split(t32[rows])
    for copy in fit:
        copy.wait()
    for row in (0, HALF):
        rows = slice(row, row + HALF)
        b_hi[rows], b_lo[rows] = split(b32[rows])
        g_hi[rows], g_lo[rows] = split(product((b_hi[rows], b_lo[rows]), (t_hi[...], t_lo[...]), NN))
    copies = []
    for far in (1, 0):
        half = (zh + far) % NZH
        rows = pl.ds(pl.multiple_of(half * HALF, HALF), HALF)
        total[far] = product((g_hi[rows], g_lo[rows]), (b_hi[...], b_lo[...]), NT)
        for k in range(NX):
            block = ((x + k) % NX) * 2
            for n, c in enumerate((core, 1 - core)):
                row = pl.multiple_of((block + c) * ROWS, 8)
                copies.append(
                    pltpu.make_async_copy(
                        total.at[far, pl.ds(row, ROWS)], outs[2 * (1 - far) + n].at[k], out_sem.at[far, n, k]
                    )
                )
                copies[-1].start()
    for copy in copies:
        copy.wait()


def call(kernel, outs, out_specs, scratch, args, in_specs, flops, moved, name):
    return pl.pallas_call(
        kernel,
        out_shape=outs,
        in_specs=in_specs,
        out_specs=out_specs,
        scratch_shapes=scratch,
        compiler_params=pltpu.CompilerParams(vmem_limit_bytes=52 * 1024 * 1024),
        cost_estimate=pl.CostEstimate(flops=flops, bytes_accessed=moved, transcendentals=0),
        name=name,
    )(*args)


def per_device(amplitudes, fitting):
    pair, aux = lax.axis_index("pair"), lax.axis_index("aux")
    place = jnp.stack([pair // NY, pair % NY, aux // 8, aux // 2 % NX, aux % 2]).astype(jnp.int32)
    fit = fitting.reshape(ROWS, V)

    def up(value):
        return pair_permute(value, lambda zl, y: (zl, y + 1))

    def down(value):
        return pair_permute(value, lambda zl, y: (zl, y - 1))

    def beside_x(value):
        return aux_permute(value, lambda zh, x, c: (zh, x + 1 - 2 * c, c))

    def pack(*parts):
        return jnp.concatenate(parts)

    tie = lax.optimization_barrier
    amp = amplitudes.reshape(ROWS, V)
    with jax.named_scope("gather"):
        near = pair_permute(fit, lambda zl, y: (zl ^ 1, y))
        two = pair_permute(fit, lambda zl, y: (zl ^ 2, y))
        own = pack(amp, swap_core(amp))
        fit_0 = up(fit), down(fit)
        beside = beside_x(own)
        amp_late, near, two = tie((amp, near, two))
        far = aux_permute(amp_late, lambda zh, x, c: (1 - zh, x, c))
        three = pair_permute(two, lambda zl, y: (zl ^ 1, y))
        beside, fit_0, near, two = tie((beside, fit_0, near, two))

        both = pack(near, two)
        below, above = up(both), down(both)
        low = up(fit_0[0])
        low, below, above, three, far = tie((low, below, above, three, far))

        far_amp, far = far, pack(far, swap_core(far))
        beside_far, beside = tie((beside_x(far), beside))
        up3 = up(pack(three, below[ROWS:]))
        down3 = down(pack(three, above[:ROWS]))
        across3 = pair_permute(three, lambda zl, y: (zl, y + 2))
        relay = aux_permute(pack(amp, far_amp), lambda zh, x, c: (zh, x + 2, c))
        amps = [own, far, beside, beside_far, swap_core(beside), swap_core(beside_far), relay, swap_core(relay)]
        fits = [fit, *fit_0, low, both, below, above, three, up3, down3, across3]

    blocks = jax.ShapeDtypeStruct((NX, ROWS, V), jnp.float32)
    vmem = pltpu.VMEM
    sems = pltpu.SemaphoreType.DMA
    far_keep, far_send, near_keep, near_send = call(
        ladder_kernel,
        (blocks,) * 4,
        (ANY,) * 4,
        [vmem((V, V), jnp.float32)] * 2
        + [vmem((V, V), jnp.bfloat16)] * 6
        + [vmem((2, HALF, V), jnp.float32), sems((32,)), sems((2, 2, NX))],
        (place, *amps, *fits),
        [SMEM] + [ANY] * 19,
        12 * V**3,
        16 * V * V,
        "ladder",
    )

    def reduce_x(keep, send):
        both = keep + swap_core(send)
        total = both[0]
        for k in (1, 2, 3):
            total = total + aux_permute(both[k], lambda zh, x, c, k=k: (zh, x + k, c))
        return total

    with jax.named_scope("reduce"):
        far_sum = aux_permute(reduce_x(far_keep, far_send), lambda zh, x, c: (1 - zh, x, c))
        result = reduce_x(near_keep, near_send) + far_sum
    return result.reshape(ROWS, 1, V)


def solution(mesh):
    in_specs = (P("aux", "pair", None), P("aux", "pair", None))
    out_specs = P("aux", "pair", None)
    return jax.shard_map(
        per_device, mesh=mesh, in_specs=in_specs, out_specs=out_specs, check_vma=False
    )
```

```python
import jax
import jax.numpy as jnp
from jax import lax
from jax.experimental import pallas as pl
from jax.experimental.pallas import tpu as pltpu
from jax.sharding import PartitionSpec as P

NZL, NY, NZH, NX, NC = 4, 4, 2, 4, 2
V = 896
HALF = 448
ROWS = 56
NN = (((1,), (0,)), ((), ()))
NT = (((1,), (1,)), ((), ()))
ANY = pl.BlockSpec(memory_space=pl.ANY)
SMEM = pl.BlockSpec(memory_space=pltpu.SMEM)


def pair_permute(value, target):
    steps = []
    for zl in range(NZL):
        for y in range(NY):
            tz, ty = target(zl, y)
            steps.append((zl * NY + y, (tz % NZL) * NY + ty % NY))
    return lax.ppermute(value, "pair", steps)


def aux_permute(value, target):
    steps = []
    for zh in range(NZH):
        for x in range(NX):
            for c in range(NC):
                th, tx, tc = target(zh, x, c)
                steps.append(((zh * NX + x) * NC + c, ((th % NZH) * NX + tx % NX) * NC + tc % NC))
    return lax.ppermute(value, "aux", steps)


def swap_core(value):
    return aux_permute(value, lambda zh, x, c: (zh, x, 1 - c))


def split(value):
    high = value.astype(jnp.bfloat16)
    low = (value - high.astype(jnp.float32)).astype(jnp.bfloat16)
    return high, low


def product(left, right, dims):
    def dot(a, b):
        return lax.dot_general(a, b, dims, preferred_element_type=jnp.float32)

    return dot(left[1], right[0]) + dot(left[0], right[1]) + dot(left[0], right[0])


def run_copies(copies):
    for copy in copies:
        copy.start()
    for copy in copies:
        copy.wait()


def fit_copies(places, target, zl, y, sem, first):
    copies = []
    for index, (ref, part, k, j) in enumerate(places):
        row = pl.multiple_of(((zl ^ k) * NY + (y + j) % NY) * ROWS, 8)
        copies.append(
            pltpu.make_async_copy(ref.at[pl.ds(part * ROWS, ROWS)], target.at[pl.ds(row, ROWS)], sem.at[first + index])
        )
    return copies


def amp_copies(refs, target, zh, x, core, sem):
    own, far, beside, beside_far, across, across_far, relay, relay_other = refs
    step = 2 * core - 1
    places = []
    for f, here, there, back in ((0, own, beside, across), (1, far, beside_far, across_far)):
        places += [(here, 0, f, 0, core), (here, 1, f, 0, 1 - core)]
        places += [(there, 0, f, step, core), (there, 1, f, step, 1 - core)]
        places += [(back, 0, f, -step, 1 - core), (back, 1, f, -step, core)]
        places += [(relay, f, f, 2, core), (relay_other, f, f, 2, 1 - core)]
    copies = []
    for index, (ref, part, f, dx, c) in enumerate(places):
        row = pl.multiple_of((((zh + f) % NZH) * 8 + ((x + dx + NX) % NX) * 2 + c) * ROWS, 8)
        copies.append(
            pltpu.make_async_copy(ref.at[pl.ds(part * ROWS, ROWS)], target.at[pl.ds(row, ROWS)], sem.at[index])
        )
    return copies


def ladder_kernel(place_ref, *refs):
    t_refs, own = refs[:8], refs[8:12]
    both, below, above, three, up3, down3, across3 = refs[12:19]
    outs = refs[19:23]
    t32, b32, t_hi, t_lo, b_hi, b_lo, g_hi, g_lo, total, sem, out_sem = refs[23:]
    zl, y, zh, x, core = (place_ref[i] for i in range(5))
    places = [(ref, 0, 0, j) for ref, j in zip(own, (0, 3, 1, 2))]
    for part in (0, 1):
        places += [(both, part, part + 1, 0), (below, part, part + 1, 3), (above, part, part + 1, 1)]
    places += [(three, 0, 3, 0), (up3, 0, 3, 3), (up3, 1, 2, 2), (down3, 0, 3, 1), (down3, 1, 1, 2), (across3, 0, 3, 2)]
    amp = amp_copies(t_refs, t32, zh, x, core, sem)
    fit = fit_copies(places, b32, zl, y, sem, 16)
    for copy in amp + fit:
        copy.start()
    for f in (0, 1):
        for copy in amp[8 * f : 8 * f + 8]:
            copy.wait()
        start = (zh + f) % NZH * HALF
        for row in range(0, HALF, 64):
            rows = pl.ds(pl.multiple_of(start + row, 64), 64)
            t_hi[rows], t_lo[rows] = split(t32[rows])
    for copy in fit:
        copy.wait()
    for row in (0, HALF):
        rows = slice(row, row + HALF)
        b_hi[rows], b_lo[rows] = split(b32[rows])
        g_hi[rows], g_lo[rows] = split(product((b_hi[rows], b_lo[rows]), (t_hi[...], t_lo[...]), NN))
    copies = []
    for far in (1, 0):
        half = (zh + far) % NZH
        rows = pl.ds(pl.multiple_of(half * HALF, HALF), HALF)
        total[far] = product((g_hi[rows], g_lo[rows]), (b_hi[...], b_lo[...]), NT)
        for k in range(NX):
            block = ((x + k) % NX) * 2
            for n, c in enumerate((core, 1 - core)):
                row = pl.multiple_of((block + c) * ROWS, 8)
                copies.append(
                    pltpu.make_async_copy(
                        total.at[far, pl.ds(row, ROWS)], outs[2 * (1 - far) + n].at[k], out_sem.at[far, n, k]
                    )
                )
                copies[-1].start()
    for copy in copies:
        copy.wait()


def call(kernel, outs, out_specs, scratch, args, in_specs, flops, moved, name):
    return pl.pallas_call(
        kernel,
        out_shape=outs,
        in_specs=in_specs,
        out_specs=out_specs,
        scratch_shapes=scratch,
        compiler_params=pltpu.CompilerParams(vmem_limit_bytes=52 * 1024 * 1024),
        cost_estimate=pl.CostEstimate(flops=flops, bytes_accessed=moved, transcendentals=0),
        name=name,
    )(*args)


def per_device(amplitudes, fitting):
    pair, aux = lax.axis_index("pair"), lax.axis_index("aux")
    place = jnp.stack([pair // NY, pair % NY, aux // 8, aux // 2 % NX, aux % 2]).astype(jnp.int32)
    fit = fitting.reshape(ROWS, V)

    def up(value):
        return pair_permute(value, lambda zl, y: (zl, y + 1))

    def down(value):
        return pair_permute(value, lambda zl, y: (zl, y - 1))

    def beside_x(value):
        return aux_permute(value, lambda zh, x, c: (zh, x + 1 - 2 * c, c))

    def pack(*parts):
        return jnp.concatenate(parts)

    tie = lax.optimization_barrier
    amp = amplitudes.reshape(ROWS, V)
    with jax.named_scope("gather"):
        near = pair_permute(fit, lambda zl, y: (zl ^ 1, y))
        two = pair_permute(fit, lambda zl, y: (zl ^ 2, y))
        own = pack(amp, swap_core(amp))
        fit_0 = up(fit), down(fit)
        beside = beside_x(own)
        amp_late, near, two = tie((amp, near, two))
        far = aux_permute(amp_late, lambda zh, x, c: (1 - zh, x, c))
        three = pair_permute(two, lambda zl, y: (zl ^ 1, y))
        beside, fit_0, near, two = tie((beside, fit_0, near, two))

        both = pack(near, two)
        below, above = up(both), down(both)
        low = up(fit_0[0])
        low, below, above, three, far = tie((low, below, above, three, far))

        far_amp, far = far, pack(far, swap_core(far))
        beside_far, beside = tie((beside_x(far), beside))
        up3 = up(pack(three, below[ROWS:]))
        down3 = down(pack(three, above[:ROWS]))
        across3 = pair_permute(three, lambda zl, y: (zl, y + 2))
        relay = aux_permute(pack(amp, far_amp), lambda zh, x, c: (zh, x + 2, c))
        amps = [own, far, beside, beside_far, swap_core(beside), swap_core(beside_far), relay, swap_core(relay)]
        fits = [fit, *fit_0, low, both, below, above, three, up3, down3, across3]

    blocks = jax.ShapeDtypeStruct((NX, ROWS, V), jnp.float32)
    vmem = pltpu.VMEM
    sems = pltpu.SemaphoreType.DMA
    far_keep, far_send, near_keep, near_send = call(
        ladder_kernel,
        (blocks,) * 4,
        (ANY,) * 4,
        [vmem((V, V), jnp.float32)] * 2
        + [vmem((V, V), jnp.bfloat16)] * 6
        + [vmem((2, HALF, V), jnp.float32), sems((32,)), sems((2, 2, NX))],
        (place, *amps, *fits),
        [SMEM] + [ANY] * 19,
        12 * V**3,
        16 * V * V,
        "ladder",
    )

    def reduce_x(keep, send):
        got = swap_core(send)
        total = keep[0] + got[0]
        for k in (1, 2, 3):
            total = total + aux_permute(keep[k] + got[k], lambda zh, x, c, k=k: (zh, x + k, c))
        return total

    with jax.named_scope("reduce"):
        far_sum = aux_permute(reduce_x(far_keep, far_send), lambda zh, x, c: (1 - zh, x, c))
        result = reduce_x(near_keep, near_send) + far_sum
    return result.reshape(ROWS, 1, V)


def solution(mesh):
    in_specs = (P("aux", "pair", None), P("aux", "pair", None))
    out_specs = P("aux", "pair", None)
    return jax.shard_map(
        per_device, mesh=mesh, in_specs=in_specs, out_specs=out_specs, check_vma=False
    )
```

```python
import jax
import jax.numpy as jnp
from jax import lax
from jax.experimental import pallas as pl
from jax.experimental.pallas import tpu as pltpu
from jax.sharding import PartitionSpec as P

NZL, NY, NZH, NX, NC = 4, 4, 2, 4, 2
V = 896
HALF = 448
ROWS = 56
NN = (((1,), (0,)), ((), ()))
NT = (((1,), (1,)), ((), ()))
ANY = pl.BlockSpec(memory_space=pl.ANY)
SMEM = pl.BlockSpec(memory_space=pltpu.SMEM)


def pair_permute(value, target):
    steps = []
    for zl in range(NZL):
        for y in range(NY):
            tz, ty = target(zl, y)
            steps.append((zl * NY + y, (tz % NZL) * NY + ty % NY))
    return lax.ppermute(value, "pair", steps)


def aux_permute(value, target):
    steps = []
    for zh in range(NZH):
        for x in range(NX):
            for c in range(NC):
                th, tx, tc = target(zh, x, c)
                steps.append(((zh * NX + x) * NC + c, ((th % NZH) * NX + tx % NX) * NC + tc % NC))
    return lax.ppermute(value, "aux", steps)


def swap_core(value):
    return aux_permute(value, lambda zh, x, c: (zh, x, 1 - c))


def split(value):
    high = value.astype(jnp.bfloat16)
    low = (value - high.astype(jnp.float32)).astype(jnp.bfloat16)
    return high, low


def product(left, right, dims):
    def dot(a, b):
        return lax.dot_general(a, b, dims, preferred_element_type=jnp.float32)

    return dot(left[1], right[0]) + dot(left[0], right[1]) + dot(left[0], right[0])


def run_copies(copies):
    for copy in copies:
        copy.start()
    for copy in copies:
        copy.wait()


def fit_copies(places, target, zl, y, sem, first):
    copies = []
    for index, (ref, part, k, j) in enumerate(places):
        row = pl.multiple_of(((zl ^ k) * NY + (y + j) % NY) * ROWS, 8)
        copies.append(
            pltpu.make_async_copy(ref.at[pl.ds(part * ROWS, ROWS)], target.at[pl.ds(row, ROWS)], sem.at[first + index])
        )
    return copies


def amp_copies(refs, target, zh, x, core, sem):
    own, far, beside, beside_far, across, across_far, relay, relay_other = refs
    step = 2 * core - 1
    places = []
    for f, here, there, back in ((0, own, beside, across), (1, far, beside_far, across_far)):
        places += [(here, 0, f, 0, core), (here, 1, f, 0, 1 - core)]
        places += [(there, 0, f, step, core), (there, 1, f, step, 1 - core)]
        places += [(back, 0, f, -step, 1 - core), (back, 1, f, -step, core)]
        places += [(relay, f, f, 2, core), (relay_other, f, f, 2, 1 - core)]
    copies = []
    for index, (ref, part, f, dx, c) in enumerate(places):
        row = pl.multiple_of((((zh + f) % NZH) * 8 + ((x + dx + NX) % NX) * 2 + c) * ROWS, 8)
        copies.append(
            pltpu.make_async_copy(ref.at[pl.ds(part * ROWS, ROWS)], target.at[pl.ds(row, ROWS)], sem.at[index])
        )
    return copies


def ladder_kernel(place_ref, *refs):
    t_refs, own = refs[:8], refs[8:12]
    both, below, above, three, up3, down3, across3 = refs[12:19]
    outs = refs[19:23]
    t32, b32, t_hi, t_lo, b_hi, b_lo, g_hi, g_lo, total, sem, out_sem = refs[23:]
    zl, y, zh, x, core = (place_ref[i] for i in range(5))
    places = [(ref, 0, 0, j) for ref, j in zip(own, (0, 3, 1, 2))]
    for part in (0, 1):
        places += [(both, part, part + 1, 0), (below, part, part + 1, 3), (above, part, part + 1, 1)]
    places += [(three, 0, 3, 0), (up3, 0, 3, 3), (up3, 1, 2, 2), (down3, 0, 3, 1), (down3, 1, 1, 2), (across3, 0, 3, 2)]
    amp = amp_copies(t_refs, t32, zh, x, core, sem)
    fit = fit_copies(places, b32, zl, y, sem, 16)
    for copy in amp + fit:
        copy.start()
    for copy in amp:
        copy.wait()
    for row in range(0, V, 128):
        rows = slice(row, row + 128)
        t_hi[rows], t_lo[rows] = split(t32[rows])
    for copy in fit:
        copy.wait()
    for row in (0, HALF):
        rows = slice(row, row + HALF)
        b_hi[rows], b_lo[rows] = split(b32[rows])
        g_hi[rows], g_lo[rows] = split(product((b_hi[rows], b_lo[rows]), (t_hi[...], t_lo[...]), NN))
    copies = []
    for far in (1, 0):
        half = (zh + far) % NZH
        rows = pl.ds(pl.multiple_of(half * HALF, HALF), HALF)
        total[far] = product((g_hi[rows], g_lo[rows]), (b_hi[...], b_lo[...]), NT)
        for k in range(NX):
            block = ((x + k) % NX) * 2
            for n, c in enumerate((core, 1 - core)):
                row = pl.multiple_of((block + c) * ROWS, 8)
                copies.append(
                    pltpu.make_async_copy(
                        total.at[far, pl.ds(row, ROWS)], outs[2 * (1 - far) + n].at[k], out_sem.at[far, n, k]
                    )
                )
                copies[-1].start()
    for copy in copies:
        copy.wait()


def call(kernel, outs, out_specs, scratch, args, in_specs, flops, moved, name):
    return pl.pallas_call(
        kernel,
        out_shape=outs,
        in_specs=in_specs,
        out_specs=out_specs,
        scratch_shapes=scratch,
        compiler_params=pltpu.CompilerParams(vmem_limit_bytes=51 * 1024 * 1024),
        cost_estimate=pl.CostEstimate(flops=flops, bytes_accessed=moved, transcendentals=0),
        name=name,
    )(*args)


def per_device(amplitudes, fitting):
    pair, aux = lax.axis_index("pair"), lax.axis_index("aux")
    place = jnp.stack([pair // NY, pair % NY, aux // 8, aux // 2 % NX, aux % 2]).astype(jnp.int32)
    fit = fitting.reshape(ROWS, V)

    def up(value):
        return pair_permute(value, lambda zl, y: (zl, y + 1))

    def down(value):
        return pair_permute(value, lambda zl, y: (zl, y - 1))

    def beside_x(value):
        return aux_permute(value, lambda zh, x, c: (zh, x + 1 - 2 * c, c))

    def pack(*parts):
        return jnp.concatenate(parts)

    tie = lax.optimization_barrier
    amp = amplitudes.reshape(ROWS, V)
    with jax.named_scope("gather"):
        near = pair_permute(fit, lambda zl, y: (zl ^ 1, y))
        two = pair_permute(fit, lambda zl, y: (zl ^ 2, y))
        own = pack(amp, swap_core(amp))
        fit_0 = up(fit), down(fit)
        beside = beside_x(own)
        amp_late, near, two = tie((amp, near, two))
        far = aux_permute(amp_late, lambda zh, x, c: (1 - zh, x, c))
        three = pair_permute(two, lambda zl, y: (zl ^ 1, y))
        beside, fit_0, near, two = tie((beside, fit_0, near, two))

        both = pack(near, two)
        below, above = up(both), down(both)
        low = up(fit_0[0])
        low, below, above, three, far = tie((low, below, above, three, far))

        far_amp, far = far, pack(far, swap_core(far))
        beside_far, beside = tie((beside_x(far), beside))
        up3 = up(pack(three, below[ROWS:]))
        down3 = down(pack(three, above[:ROWS]))
        across3 = pair_permute(three, lambda zl, y: (zl, y + 2))
        relay = aux_permute(pack(amp, far_amp), lambda zh, x, c: (zh, x + 2, c))
        amps = [own, far, beside, beside_far, swap_core(beside), swap_core(beside_far), relay, swap_core(relay)]
        fits = [fit, *fit_0, low, both, below, above, three, up3, down3, across3]

    blocks = jax.ShapeDtypeStruct((NX, ROWS, V), jnp.float32)
    vmem = pltpu.VMEM
    sems = pltpu.SemaphoreType.DMA
    far_keep, far_send, near_keep, near_send = call(
        ladder_kernel,
        (blocks,) * 4,
        (ANY,) * 4,
        [vmem((V, V), jnp.float32)] * 2
        + [vmem((V, V), jnp.bfloat16)] * 6
        + [vmem((2, HALF, V), jnp.float32), sems((32,)), sems((2, 2, NX))],
        (place, *amps, *fits),
        [SMEM] + [ANY] * 19,
        12 * V**3,
        16 * V * V,
        "ladder",
    )

    def reduce_x(keep, send):
        both = keep + swap_core(send)
        total = both[0]
        for k in (1, 2, 3):
            total = total + aux_permute(both[k], lambda zh, x, c, k=k: (zh, x + k, c))
        return total

    with jax.named_scope("reduce"):
        far_sum = aux_permute(reduce_x(far_keep, far_send), lambda zh, x, c: (1 - zh, x, c))
        result = reduce_x(near_keep, near_send) + far_sum
    return result.reshape(ROWS, 1, V)


def solution(mesh):
    in_specs = (P("aux", "pair", None), P("aux", "pair", None))
    out_specs = P("aux", "pair", None)
    return jax.shard_map(
        per_device, mesh=mesh, in_specs=in_specs, out_specs=out_specs, check_vma=False
    )
```
